32 devices in a mesh: groups: 2 (over y), fsdp: 8 (over z, x), rep: 2 (over core).
Axes of the slice: x: 2, y: 2, z: 4, core: 2. Of those that a mesh axis runs over, the one named last changes fastest.
Arguments:
- weights: bfloat16 [448, 128, 1024], P(('groups', 'fsdp'), None, 'rep'), parts along dimension 0
- block_ids: int32 [224], replicated, may hold values from 0 to 223, as said below
- owner_map: int32 [8], replicated, may hold values from 0 to 7, each once
Outputs:
- quantized: bfloat16 [16, 1024, 3584], P(('groups', 'fsdp')), parts along dimension 0
- scales: bfloat16 [16, 8, 28], P(('groups', 'fsdp')), parts along dimension 0
The draws below stay inside these ranges and needn't reach their ends.
There are 2 independent parts, one for each index of `groups`. The reference program is written for one: setup_inputs(seed, part) draws one part's arguments, and reference() takes and returns one part's arrays. A program takes and returns all parts, laid end to end along the dimension named above; an argument that names none is the same for every part. Nothing has to cross between parts.
Inputs may be any that keep to these rules, and one draw needn't show every extreme that they name: block_ids names every one of the 224 blocks once; each device's 28 slots hold one block of each block row j, and at most 4 blocks of any one expert, a number that some device reaches. `owner_map`: every device along fsdp owns exactly one expert.
All inputs are finite; a program needn't handle non-finite values.
Results may differ from the reference program's by a relative error of at most 0.001.
Values may be sent and summed in bfloat16 or wider, within the bound.
A program may use at most 128 MiB of HBM per device.

```python
import math
import jax
import jax.numpy as jnp
from jax import lax

D = 3584
FF = 1024
BPE = 28
EXPERTS = 8
SLOTS = 224


def draw_weights(key, part):
    key = jax.random.fold_in(key, 11)
    first, second, third = jax.random.split(key, 3)
    base = jax.random.normal(first, (SLOTS, 128, FF), jnp.float32)
    spread = math.log(10.0)
    row_scale = jnp.exp(jax.random.uniform(second, (SLOTS, 128, 1), jnp.float32) * spread)
    col_scale = jnp.exp(jax.random.uniform(third, (1, 1, FF), jnp.float32) * spread)
    return (base * row_scale * col_scale * (0.25 / math.sqrt(D))).astype(jnp.bfloat16)


def draw_block_ids(key, part):
    key = jax.random.fold_in(key, 5)
    first, second, third = jax.random.split(key, 3)
    offsets = jax.random.permutation(first, EXPERTS).astype(jnp.int32)
    relabel = jax.random.permutation(second, EXPERTS).astype(jnp.int32)
    inverse = jnp.zeros((EXPERTS,), jnp.int32).at[relabel].set(jnp.arange(EXPERTS, dtype=jnp.int32))
    row_order = jax.vmap(lambda sub: jax.random.permutation(sub, BPE))(jax.random.split(third, EXPERTS)).astype(jnp.int32)
    device = jnp.arange(EXPERTS, dtype=jnp.int32)[:, None]
    expert = (inverse[device] - offsets[row_order % EXPERTS]) % EXPERTS
    return (expert * BPE + row_order).reshape(SLOTS).astype(jnp.int32)


def setup_inputs(seed: int = 0, part: int = 0) -> dict:
    key_list = jax.random.split(jax.random.key(seed), 4)
    part_keys = jax.random.split(jax.random.fold_in(key_list[3], part), 4)
    weights = draw_weights(jax.random.fold_in(jax.random.fold_in(key_list[3], part), 71), part)
    block_ids = draw_block_ids(jax.random.fold_in(key_list[3], 71), part)
    owner_map = jax.random.permutation(key_list[2], EXPERTS).astype(jnp.int32)
    return {"weights": weights, "block_ids": block_ids, "owner_map": owner_map}


def quantize(blocks):
    amount, height, breadth = blocks.shape
    widened = blocks.astype(jnp.float32).reshape(amount, height, breadth // 128, 128)
    largest = jnp.max(jnp.abs(widened), axis=(1, 3))
    block_scale = (largest + 1e-6).astype(jnp.bfloat16)
    divided = widened / block_scale.astype(jnp.float32)[:, None, :, None]
    return divided.astype(jnp.bfloat16).reshape(amount, height, breadth), block_scale


def reference(weights, block_ids, owner_map):
    slot_of_block = jnp.zeros((SLOTS,), jnp.int32).at[block_ids].set(jnp.arange(SLOTS, dtype=jnp.int32))
    expert_of_owner = jnp.zeros((EXPERTS,), jnp.int32).at[owner_map].set(jnp.arange(EXPERTS, dtype=jnp.int32))

    def one_owner(owner_index):
        expert = expert_of_owner[owner_index]
        slot_list = lax.dynamic_slice_in_dim(slot_of_block, (expert * BPE).astype(jnp.int32), BPE)
        blocks = weights[slot_list]
        scaled, block_scale = quantize(blocks)
        return scaled.reshape(D, FF).T, block_scale.T

    quantized, scales = lax.map(one_owner, jnp.arange(EXPERTS, dtype=jnp.int32))
    return quantized, scales
```

```python
import functools

import jax
import jax.numpy as jnp
from jax import lax
from jax.experimental import pallas as pl
from jax.experimental.pallas import tpu as pltpu
from jax.sharding import PartitionSpec as P

MESH = pl.DeviceIdType.MESH
LANES = 128


def far_first(step, shards):
    distance = (step + 1) // 2
    sign = 1 - 2 * ((step + 1) % 2)
    return (shards // 2 + sign * distance + shards) % shards


def exchange_kernel(
    shards, capacity, source_ref, weights_ref, landed_ref, outgoing, send_sem, recv_sem, pass_sem, passed_sem
):
    me = lax.axis_index("fsdp")
    core = lax.axis_index("rep")
    other = 1 - core
    columns = weights_ref.shape[2]
    tiles = columns // LANES
    block_rows = capacity * columns

    barrier = pltpu.get_barrier_semaphore()

    def greet(step, carry):
        peer = (me + step) % shards
        pl.semaphore_signal(barrier, inc=1, device_id={"fsdp": peer}, device_id_type=MESH)
        return carry

    lax.fori_loop(1, shards, greet, 0)
    pl.semaphore_signal(barrier, inc=1, device_id={"rep": other}, device_id_type=MESH)
    pl.semaphore_wait(barrier, shards)

    def fill(owner):
        scale_rows = outgoing.shape[1] - block_rows
        row_ids = lax.broadcasted_iota(jnp.int32, (scale_rows, LANES), 0)
        scale_tile = jnp.zeros((scale_rows, LANES), jnp.float32)
        for slot in range(capacity):
            source = source_ref[owner * capacity + slot]
            for tile in range(tiles):
                block = weights_ref[source, :, tile * LANES : (tile + 1) * LANES].astype(jnp.float32)
                largest = jnp.max(jnp.max(jnp.abs(block), axis=0, keepdims=True), axis=1, keepdims=True)
                scale = (largest + 1e-06).astype(jnp.bfloat16).astype(jnp.float32)
                divided = (block / scale).astype(jnp.bfloat16)
                start = (slot * tiles + tile) * LANES
                outgoing[owner, start : start + LANES, :] = divided.T
                scale_tile = jnp.where(row_ids == slot * tiles + tile, scale, scale_tile)
        outgoing[owner, block_rows:, :] = scale_tile.astype(jnp.bfloat16)

    def to_owner(owner):
        return pltpu.make_async_remote_copy(
            src_ref=outgoing.at[owner],
            dst_ref=landed_ref.at[core, me],
            send_sem=send_sem.at[owner],
            recv_sem=recv_sem.at[me],
            device_id={"fsdp": owner},
            device_id_type=MESH,
        )

    def from_sender(sender):
        return pltpu.make_async_remote_copy(
            src_ref=outgoing.at[sender],
            dst_ref=landed_ref.at[core, sender],
            send_sem=send_sem.at[sender],
            recv_sem=recv_sem.at[sender],
            device_id={"fsdp": sender},
            device_id_type=MESH,
        )

    def to_core(sender):
        return pltpu.make_async_remote_copy(
            src_ref=landed_ref.at[core, sender],
            dst_ref=landed_ref.at[core, sender],
            send_sem=pass_sem.at[sender],
            recv_sem=passed_sem.at[sender],
            device_id={"rep": other},
            device_id_type=MESH,
        )

    def from_core(sender):
        return pltpu.make_async_remote_copy(
            src_ref=landed_ref.at[other, sender],
            dst_ref=landed_ref.at[other, sender],
            send_sem=pass_sem.at[sender],
            recv_sem=passed_sem.at[sender],
            device_id={"rep": other},
            device_id_type=MESH,
        )

    def send(step, carry):
        owner = (me + far_first(step, shards)) % shards
        fill(owner)
        to_owner(owner).start()
        return carry

    lax.fori_loop(0, shards - 1, send, 0)
    fill(me)
    keep = pltpu.make_async_copy(outgoing.at[me], landed_ref.at[core, me], recv_sem.at[me])
    keep.start()
    keep.wait()
    to_core(me).start()

    def forward(step, carry):
        sender = (me - far_first(step, shards) + shards) % shards
        from_sender(sender).wait_recv()
        to_core(sender).start()
        return carry

    lax.fori_loop(0, shards - 1, forward, 0)

    def finish(step, carry):
        peer = (me + step) % shards
        to_owner(peer).wait_send()
        return carry

    lax.fori_loop(1, shards, finish, 0)

    def finish_core(sender, carry):
        to_core(sender).wait_send()
        from_core(sender).wait_recv()
        return carry

    lax.fori_loop(0, shards, finish_core, 0)


def place_kernel(capacity, columns, pick_ref, landed_ref, matrix_ref, scales_ref, scale_tiles, scale_sem, sems):
    cores, shards, rows, _ = landed_ref.shape
    per_device = pick_ref.shape[0]
    tiles = columns // LANES
    block_rows = capacity * columns
    scale_copy = pltpu.make_async_copy(
        landed_ref.at[:, :, pl.ds(block_rows, rows - block_rows), :], scale_tiles, scale_sem
    )
    scale_copy.start()

    def move(index, half):
        picked = pick_ref[index]
        sender, slot = picked // capacity, picked % capacity
        return pltpu.make_async_copy(
            landed_ref.at[half, sender, pl.ds(pl.multiple_of(slot * columns, columns), columns), :],
            matrix_ref.at[0, pl.ds(half * columns, columns), pl.ds(pl.multiple_of(index * LANES, LANES), LANES)],
            sems.at[half, index],
        )

    def begin(index, carry):
        for half in range(cores):
            move(index, half).start()
        return carry

    lax.fori_loop(0, per_device, begin, 0)
    scale_copy.wait()
    lanes = lax.broadcasted_iota(jnp.int32, (rows - block_rows, LANES), 1)
    rows_of = lax.broadcasted_iota(jnp.int32, (rows - block_rows, LANES), 0)

    def gather(index, totals):
        picked = pick_ref[index]
        sender, slot = picked // capacity, picked % capacity
        hit = (lanes == index) & (rows_of // tiles == slot)
        return tuple(
            jnp.where(hit, scale_tiles[half, sender].astype(jnp.float32), totals[half]) for half in range(cores)
        )

    zero = jnp.zeros((rows - block_rows, LANES), jnp.float32)
    totals = lax.fori_loop(0, per_device, gather, (zero,) * cores)
    for half in range(cores):
        folded = jnp.zeros((tiles, LANES), jnp.float32)
        for slot in range(capacity):
            folded = folded + totals[half][slot * tiles : (slot + 1) * tiles]
        scales_ref[0, half * tiles : (half + 1) * tiles, :] = folded[:, :per_device].astype(jnp.bfloat16)

    def end(index, carry):
        for half in range(cores):
            move(index, half).wait()
        return carry

    lax.fori_loop(0, per_device, end, 0)


def body(weights, block_ids, owner_map):
    shards = lax.axis_size("fsdp")
    cores = lax.axis_size("rep")
    myself = lax.axis_index("fsdp")
    per_device, height, columns = weights.shape
    experts_total = owner_map.shape[0]
    capacity = (per_device + shards - 1) // shards
    layout = block_ids.reshape(shards, per_device)
    expert_ids = jnp.arange(experts_total, dtype=jnp.int32)
    local_ids = jnp.arange(per_device, dtype=jnp.int32)
    holder = layout // per_device
    earlier = local_ids[None, :] < local_ids[:, None]

    mine = lax.dynamic_index_in_dim(holder, myself, 0, keepdims=False)
    my_owner = jnp.sum(jnp.where(mine[:, None] == expert_ids, owner_map, 0), axis=1)
    my_rank = jnp.sum(jnp.where((mine[:, None] == mine[None, :]) & earlier, 1, 0), axis=1)
    places = jnp.arange(shards * capacity, dtype=jnp.int32)
    source = jnp.sum(jnp.where((my_owner * capacity + my_rank)[None, :] == places[:, None], local_ids[None, :], 0), axis=1)

    my_expert = jnp.sum(jnp.where(owner_map == myself, expert_ids, 0))
    held = holder == my_expert
    ranking = jnp.sum(jnp.where(held[:, None, :] & earlier[None], 1, 0), axis=2)
    received_at = jnp.arange(shards, dtype=jnp.int32)[:, None] * capacity + ranking
    matches = layout[None, :, :] == (my_expert * per_device + local_ids)[:, None, None]
    picking = jnp.sum(jnp.where(matches, received_at[None], 0), axis=(1, 2))

    tiles = columns // LANES
    scale_rows = (capacity * tiles + 15) // 16 * 16
    rows = capacity * columns + scale_rows
    landed = pl.pallas_call(
        functools.partial(exchange_kernel, shards, capacity),
        out_shape=jax.ShapeDtypeStruct((cores, shards, rows, LANES), jnp.bfloat16),
        in_specs=[pl.BlockSpec(memory_space=pltpu.SMEM), pl.BlockSpec(memory_space=pltpu.VMEM)],
        out_specs=pl.BlockSpec(memory_space=pl.ANY),
        scratch_shapes=[
            pltpu.VMEM((shards, rows, LANES), jnp.bfloat16),
            pltpu.SemaphoreType.DMA((shards,)),
            pltpu.SemaphoreType.DMA((shards,)),
            pltpu.SemaphoreType.DMA((shards,)),
            pltpu.SemaphoreType.DMA((shards,)),
        ],
        compiler_params=pltpu.CompilerParams(
            collective_id=0, has_side_effects=True, vmem_limit_bytes=48 * 1024 * 1024
        ),
        name="exchange",
    )(source, weights)
    return pl.pallas_call(
        functools.partial(place_kernel, capacity, columns),
        out_shape=(
            jax.ShapeDtypeStruct((1, cores * columns, per_device * height), jnp.bfloat16),
            jax.ShapeDtypeStruct((1, cores * tiles, per_device), jnp.bfloat16),
        ),
        in_specs=[pl.BlockSpec(memory_space=pltpu.SMEM), pl.BlockSpec(memory_space=pl.ANY)],
        out_specs=(pl.BlockSpec(memory_space=pl.ANY), pl.BlockSpec(memory_space=pltpu.VMEM)),
        scratch_shapes=[
            pltpu.VMEM((cores, shards, scale_rows, LANES), jnp.bfloat16),
            pltpu.SemaphoreType.DMA,
            pltpu.SemaphoreType.DMA((cores, per_device)),
        ],
        compiler_params=pltpu.CompilerParams(vmem_limit_bytes=48 * 1024 * 1024),
        name="place",
    )(picking, landed)


def solution(mesh):
    return jax.shard_map(
        body,
        mesh=mesh,
        in_specs=(P(("groups", "fsdp"), None, "rep"), P(), P()),
        out_specs=(P(("groups", "fsdp"), None, None), P(("groups", "fsdp"), None, None)),
        check_vma=False,
    )
```

```python
import functools

import jax
import jax.numpy as jnp
from jax import lax
from jax.experimental import pallas as pl
from jax.experimental.pallas import tpu as pltpu
from jax.sharding import PartitionSpec as P

MESH = pl.DeviceIdType.MESH
LANES = 128


def far_first(step, shards):
    distance = (step + 1) // 2
    sign = 1 - 2 * ((step + 1) % 2)
    return (shards // 2 + sign * distance + shards) % shards


def exchange_kernel(
    shards,
    capacity,
    block_ids_ref,
    owner_map_ref,
    weights_ref,
    landed_ref,
    held_weights,
    outgoing,
    owner_of,
    read_sem,
    send_sem,
    recv_sem,
    pass_sem,
    passed_sem,
):
    me = lax.axis_index("fsdp")
    core = lax.axis_index("rep")
    other = 1 - core
    per_device, _, columns = weights_ref.shape
    tiles = columns // LANES
    block_rows = capacity * columns
    read = pltpu.make_async_copy(weights_ref, held_weights, read_sem)
    read.start()

    barrier = pltpu.get_barrier_semaphore()

    def greet(step, carry):
        peer = (me + step) % shards
        pl.semaphore_signal(barrier, inc=1, device_id={"fsdp": peer}, device_id_type=MESH)
        return carry

    lax.fori_loop(1, shards, greet, 0)
    pl.semaphore_signal(barrier, inc=1, device_id={"rep": other}, device_id_type=MESH)

    def look_up(index, carry):
        owner_of[index] = owner_map_ref[lax.div(block_ids_ref[me * per_device + index], per_device)]
        return carry

    lax.fori_loop(0, per_device, look_up, 0)
    pl.semaphore_wait(barrier, shards)
    read.wait()

    def sources_for(owner):
        def step(index, carry):
            count, found = carry
            hit = owner_of[index] == owner
            found = tuple(jnp.where(hit & (count == slot), index, old) for slot, old in enumerate(found))
            return count + hit.astype(jnp.int32), found

        zero = jnp.int32(0)
        return lax.fori_loop(0, per_device, step, (zero, (zero,) * capacity))[1]

    def fill(owner):
        sources = sources_for(owner)
        scale_rows = outgoing.shape[1] - block_rows
        row_ids = lax.broadcasted_iota(jnp.int32, (scale_rows, LANES), 0)
        scale_tile = jnp.zeros((scale_rows, LANES), jnp.float32)
        for slot in range(capacity):
            source = sources[slot]
            for tile in range(tiles):
                block = held_weights[source, :, tile * LANES : (tile + 1) * LANES].astype(jnp.float32)
                largest = jnp.max(jnp.max(jnp.abs(block), axis=0, keepdims=True), axis=1, keepdims=True)
                scale = (largest + 1e-06).astype(jnp.bfloat16).astype(jnp.float32)
                divided = (block / scale).astype(jnp.bfloat16)
                start = (tile * capacity + slot) * LANES
                outgoing[owner, start : start + LANES, :] = divided.T
                scale_tile = jnp.where(row_ids == slot * tiles + tile, scale, scale_tile)
        outgoing[owner, block_rows:, :] = scale_tile.astype(jnp.bfloat16)

    def to_owner(owner):
        return pltpu.make_async_remote_copy(
            src_ref=outgoing.at[owner],
            dst_ref=landed_ref.at[core, me],
            send_sem=send_sem.at[owner],
            recv_sem=recv_sem.at[me],
            device_id={"fsdp": owner},
            device_id_type=MESH,
        )

    def from_sender(sender):
        return pltpu.make_async_remote_copy(
            src_ref=outgoing.at[sender],
            dst_ref=landed_ref.at[core, sender],
            send_sem=send_sem.at[sender],
            recv_sem=recv_sem.at[sender],
            device_id={"fsdp": sender},
            device_id_type=MESH,
        )

    def to_core(sender):
        return pltpu.make_async_remote_copy(
            src_ref=landed_ref.at[core, sender],
            dst_ref=landed_ref.at[core, sender],
            send_sem=pass_sem.at[sender],
            recv_sem=passed_sem.at[sender],
            device_id={"rep": other},
            device_id_type=MESH,
        )

    def from_core(sender):
        return pltpu.make_async_remote_copy(
            src_ref=landed_ref.at[other, sender],
            dst_ref=landed_ref.at[other, sender],
            send_sem=pass_sem.at[sender],
            recv_sem=passed_sem.at[sender],
            device_id={"rep": other},
            device_id_type=MESH,
        )

    def send(step, carry):
        owner = (me + far_first(step, shards)) % shards
        fill(owner)
        to_owner(owner).start()
        return carry

    lax.fori_loop(0, shards - 1, send, 0)
    fill(me)
    keep = pltpu.make_async_copy(outgoing.at[me], landed_ref.at[core, me], recv_sem.at[me])
    keep.start()
    keep.wait()
    to_core(me).start()

    def forward(step, carry):
        sender = (me - far_first(step, shards) + shards) % shards
        from_sender(sender).wait_recv()
        to_core(sender).start()
        return carry

    lax.fori_loop(0, shards - 1, forward, 0)

    def finish(step, carry):
        peer = (me + step) % shards
        to_owner(peer).wait_send()
        return carry

    lax.fori_loop(1, shards, finish, 0)

    def finish_core(sender, carry):
        to_core(sender).wait_send()
        from_core(sender).wait_recv()
        return carry

    lax.fori_loop(0, shards, finish_core, 0)


def place_kernel(
    capacity,
    columns,
    block_ids_ref,
    owner_map_ref,
    landed_ref,
    matrix_ref,
    scales_ref,
    pieces,
    staged,
    scale_tiles,
    pick_ref,
    read_sems,
    write_sems,
    scale_sem,
):
    me = lax.axis_index("fsdp")
    cores, shards, rows, _ = landed_ref.shape
    per_device = pick_ref.shape[0] - 1
    tiles = columns // LANES
    block_rows = capacity * columns
    piece_rows = capacity * LANES

    def read(piece):
        half, tile = piece // tiles, piece % tiles
        return pltpu.make_async_copy(
            landed_ref.at[half, :, pl.ds(tile * piece_rows, piece_rows), :], pieces.at[piece], read_sems.at[piece]
        )

    def write(piece):
        return pltpu.make_async_copy(
            staged.at[piece], matrix_ref.at[0, pl.ds(piece * LANES, LANES), :], write_sems.at[piece]
        )

    scale_copy = pltpu.make_async_copy(
        landed_ref.at[:, :, pl.ds(block_rows, rows - block_rows), :], scale_tiles, scale_sem
    )
    for piece in range(cores * tiles):
        read(piece).start()
    scale_copy.start()

    def find_expert(expert, found):
        return jnp.where(owner_map_ref[expert] == me, expert, found)

    lowest = per_device * lax.fori_loop(0, owner_map_ref.shape[0], find_expert, jnp.int32(0))

    def look_up(sender, carry):
        count = jnp.int32(0)
        for index in range(per_device):
            row = block_ids_ref[sender * per_device + index] - lowest
            hit = (row >= 0) & (row < per_device)
            pick_ref[jnp.where(hit, row, per_device)] = sender * capacity + count
            count = count + hit.astype(jnp.int32)
        return carry

    lax.fori_loop(0, shards, look_up, 0)

    for piece in range(cores * tiles):
        read(piece).wait()

        for index in range(per_device):
            picked = pick_ref[index]
            sender, slot = lax.div(picked, capacity), lax.rem(picked, capacity)
            staged[piece, :, index * LANES : (index + 1) * LANES] = pieces[
                piece, sender, pl.ds(pl.multiple_of(slot * LANES, LANES), LANES), :
            ]
        write(piece).start()
    scale_copy.wait()
    lanes = lax.broadcasted_iota(jnp.int32, (rows - block_rows, LANES), 1)
    rows_of = lax.broadcasted_iota(jnp.int32, (rows - block_rows, LANES), 0)

    def gather(index, totals):
        picked = pick_ref[index]
        sender, slot = lax.div(picked, capacity), lax.rem(picked, capacity)
        hit = (lanes == index) & (rows_of // tiles == slot)
        return tuple(
            jnp.where(hit, scale_tiles[half, sender].astype(jnp.float32), totals[half]) for half in range(cores)
        )

    zero = jnp.zeros((rows - block_rows, LANES), jnp.float32)
    totals = lax.fori_loop(0, per_device, gather, (zero,) * cores)
    for half in range(cores):
        folded = jnp.zeros((tiles, LANES), jnp.float32)
        for slot in range(capacity):
            folded = folded + totals[half][slot * tiles : (slot + 1) * tiles]
        scales_ref[0, half * tiles : (half + 1) * tiles, :] = folded[:, :per_device].astype(jnp.bfloat16)

    for piece in range(cores * tiles):
        write(piece).wait()


def body(weights, block_ids, owner_map):
    shards = lax.axis_size("fsdp")
    cores = lax.axis_size("rep")
    per_device, height, columns = weights.shape
    capacity = (per_device + shards - 1) // shards
    tiles = columns // LANES
    scale_rows = (capacity * tiles + 15) // 16 * 16
    rows = capacity * columns + scale_rows
    scalars = pl.BlockSpec(memory_space=pltpu.SMEM)
    landed = pl.pallas_call(
        functools.partial(exchange_kernel, shards, capacity),
        out_shape=jax.ShapeDtypeStruct((cores, shards, rows, LANES), jnp.bfloat16),
        in_specs=[scalars, scalars, pl.BlockSpec(memory_space=pl.ANY)],
        out_specs=pl.BlockSpec(memory_space=pl.ANY),
        scratch_shapes=[
            pltpu.VMEM(weights.shape, jnp.bfloat16),
            pltpu.VMEM((shards, rows, LANES), jnp.bfloat16),
            pltpu.SMEM((per_device,), jnp.int32),
            pltpu.SemaphoreType.DMA,
            pltpu.SemaphoreType.DMA((shards,)),
            pltpu.SemaphoreType.DMA((shards,)),
            pltpu.SemaphoreType.DMA((shards,)),
            pltpu.SemaphoreType.DMA((shards,)),
        ],
        compiler_params=pltpu.CompilerParams(
            collective_id=0, has_side_effects=True, vmem_limit_bytes=48 * 1024 * 1024
        ),
        name="exchange",
    )(block_ids, owner_map, weights)
    return pl.pallas_call(
        functools.partial(place_kernel, capacity, columns),
        out_shape=(
            jax.ShapeDtypeStruct((1, cores * columns, per_device * height), jnp.bfloat16),
            jax.ShapeDtypeStruct((1, cores * tiles, per_device), jnp.bfloat16),
        ),
        in_specs=[scalars, scalars, pl.BlockSpec(memory_space=pl.ANY)],
        out_specs=(pl.BlockSpec(memory_space=pl.ANY), pl.BlockSpec(memory_space=pltpu.VMEM)),
        scratch_shapes=[
            pltpu.VMEM((cores * tiles, shards, capacity * LANES, LANES), jnp.bfloat16),
            pltpu.VMEM((cores * tiles, LANES, per_device * height), jnp.bfloat16),
            pltpu.VMEM((cores, shards, scale_rows, LANES), jnp.bfloat16),
            pltpu.SMEM((per_device + 1,), jnp.int32),
            pltpu.SemaphoreType.DMA((cores * tiles,)),
            pltpu.SemaphoreType.DMA((cores * tiles,)),
            pltpu.SemaphoreType.DMA,
        ],
        compiler_params=pltpu.CompilerParams(vmem_limit_bytes=48 * 1024 * 1024),
        name="place",
    )(block_ids, owner_map, landed)


def solution(mesh):
    return jax.shard_map(
        body,
        mesh=mesh,
        in_specs=(P(("groups", "fsdp"), None, "rep"), P(), P()),
        out_specs=(P(("groups", "fsdp"), None, None), P(("groups", "fsdp"), None, None)),
        check_vma=False,
    )
```

```python
import functools

import jax
import jax.numpy as jnp
from jax import lax
from jax.experimental import pallas as pl
from jax.experimental.pallas import tpu as pltpu
from jax.sharding import PartitionSpec as P

MESH = pl.DeviceIdType.MESH
LANES = 128


def far_first(step, shards):
    distance = (step + 1) // 2
    sign = 1 - 2 * ((step + 1) % 2)
    return (shards // 2 + sign * distance + shards) % shards


def exchange_kernel(
    shards,
    capacity,
    block_ids_ref,
    owner_map_ref,
    weights_ref,
    landed_ref,
    landed_scales_ref,
    held_weights,
    outgoing,
    outgoing_scales,
    owner_of,
    read_sem,
    send_sem,
    recv_sem,
    pass_sem,
    passed_sem,
):
    me = lax.axis_index("fsdp")
    core = lax.axis_index("rep")
    other = 1 - core
    per_device, _, columns = weights_ref.shape
    tiles = columns // LANES
    read = pltpu.make_async_copy(weights_ref, held_weights, read_sem)
    read.start()

    barrier = pltpu.get_barrier_semaphore()

    def greet(step, carry):
        peer = (me + step) % shards
        pl.semaphore_signal(barrier, inc=1, device_id={"fsdp": peer}, device_id_type=MESH)
        return carry

    lax.fori_loop(1, shards, greet, 0)
    pl.semaphore_signal(barrier, inc=1, device_id={"rep": other}, device_id_type=MESH)

    def look_up(index, carry):
        owner_of[index] = owner_map_ref[lax.div(block_ids_ref[me * per_device + index], per_device)]
        return carry

    lax.fori_loop(0, per_device, look_up, 0)
    pl.semaphore_wait(barrier, shards)
    read.wait()

    def sources_for(owner):
        def step(index, carry):
            count, found = carry
            hit = owner_of[index] == owner
            found = tuple(jnp.where(hit & (count == slot), index, old) for slot, old in enumerate(found))
            return count + hit.astype(jnp.int32), found

        zero = jnp.int32(0)
        return lax.fori_loop(0, per_device, step, (zero, (zero,) * capacity))[1]

    def fill(owner, slot, source, scale_tile):
        row_ids = lax.broadcasted_iota(jnp.int32, scale_tile.shape, 0)
        for tile in range(tiles):
            block = held_weights[source, :, tile * LANES : (tile + 1) * LANES].astype(jnp.float32)
            largest = jnp.max(jnp.max(jnp.abs(block), axis=0, keepdims=True), axis=1, keepdims=True)
            scale = (largest + 1e-06).astype(jnp.bfloat16).astype(jnp.float32)
            divided = (block / scale).astype(jnp.bfloat16)
            outgoing[owner, slot, tile * LANES : (tile + 1) * LANES, :] = divided.T
            scale_tile = jnp.where(row_ids == slot * tiles + tile, scale, scale_tile)
        return scale_tile

    def copy(start, landing, part, device, done, arrived):
        if part < capacity:
            start_ref, landing_ref = start[0].at[start[2], part], landing[0].at[landing[2], landing[3], part]
        else:
            start_ref, landing_ref = start[1].at[start[2]], landing[1].at[landing[2], landing[3]]
        return pltpu.make_async_remote_copy(
            src_ref=start_ref,
            dst_ref=landing_ref,
            send_sem=done,
            recv_sem=arrived,
            device_id=device,
            device_id_type=MESH,
        )

    outbox = (outgoing, outgoing_scales)
    landed = (landed_ref, landed_scales_ref)

    def to_owner(owner, part):
        return copy(
            (*outbox, owner), (*landed, core, me), part, {"fsdp": owner}, send_sem.at[owner, part], recv_sem.at[me, part]
        )

    def from_sender(sender, part):
        return copy(
            (*outbox, sender),
            (*landed, core, sender),
            part,
            {"fsdp": sender},
            send_sem.at[sender, part],
            recv_sem.at[sender, part],
        )

    def between_cores(half, sender, part):
        here = (landed_ref.at[half], landed_scales_ref.at[half], sender)
        return copy(
            here,
            (*landed, half, sender),
            part,
            {"rep": other},
            pass_sem.at[sender, part],
            passed_sem.at[sender, part],
        )

    def keep(part):
        if part < capacity:
            start_ref, landing_ref = outgoing.at[me, part], landed_ref.at[core, me, part]
        else:
            start_ref, landing_ref = outgoing_scales.at[me], landed_scales_ref.at[core, me]
        return pltpu.make_async_copy(start_ref, landing_ref, recv_sem.at[me, part])

    def prepare(owner, launch):
        sources = sources_for(owner)
        scale_tile = jnp.zeros(outgoing_scales.shape[1:], jnp.float32)
        for slot in range(capacity):
            scale_tile = fill(owner, slot, sources[slot], scale_tile)
            launch(slot).start()
        outgoing_scales[owner] = scale_tile.astype(jnp.bfloat16)
        launch(capacity).start()

    parts = range(capacity + 1)

    def send(step, carry):
        owner = (me + far_first(step, shards)) % shards
        prepare(owner, functools.partial(to_owner, owner))
        return carry

    lax.fori_loop(0, shards - 1, send, 0)
    prepare(me, keep)
    for part in parts:
        keep(part).wait()
        between_cores(core, me, part).start()

    def forward(step, carry):
        sender = (me - far_first(step, shards) + shards) % shards
        for part in parts:
            from_sender(sender, part).wait_recv()
            between_cores(core, sender, part).start()
        return carry

    lax.fori_loop(0, shards - 1, forward, 0)

    def finish(step, carry):
        peer = (me + step) % shards
        for part in parts:
            to_owner(peer, part).wait_send()
        return carry

    lax.fori_loop(1, shards, finish, 0)

    def finish_core(sender, carry):
        for part in parts:
            between_cores(core, sender, part).wait_send()
            between_cores(other, sender, part).wait_recv()
        return carry

    lax.fori_loop(0, shards, finish_core, 0)


def place_kernel(
    block_ids_ref,
    owner_map_ref,
    landed_ref,
    landed_scales_ref,
    matrix_ref,
    scales_ref,
    pieces,
    staged,
    scale_tiles,
    pick_ref,
    read_sems,
    write_sems,
    scale_sem,
):
    me = lax.axis_index("fsdp")
    cores, shards, capacity, columns, _ = landed_ref.shape
    scale_rows = landed_scales_ref.shape[2]
    per_device = pick_ref.shape[0] - 1
    tiles = columns // LANES

    def read(piece):
        half, tile = piece // tiles, piece % tiles
        return pltpu.make_async_copy(
            landed_ref.at[half, :, :, pl.ds(tile * LANES, LANES), :], pieces.at[piece], read_sems.at[piece]
        )

    def write(piece):
        return pltpu.make_async_copy(
            staged.at[piece], matrix_ref.at[0, pl.ds(piece * LANES, LANES), :], write_sems.at[piece]
        )

    scale_copy = pltpu.make_async_copy(landed_scales_ref, scale_tiles, scale_sem)
    for piece in range(cores * tiles):
        read(piece).start()
    scale_copy.start()

    def find_expert(expert, found):
        return jnp.where(owner_map_ref[expert] == me, expert, found)

    lowest = per_device * lax.fori_loop(0, owner_map_ref.shape[0], find_expert, jnp.int32(0))

    def look_up(sender, carry):
        count = jnp.int32(0)
        for index in range(per_device):
            row = block_ids_ref[sender * per_device + index] - lowest
            hit = (row >= 0) & (row < per_device)
            pick_ref[jnp.where(hit, row, per_device)] = sender * capacity + count
            count = count + hit.astype(jnp.int32)
        return carry

    lax.fori_loop(0, shards, look_up, 0)

    for piece in range(cores * tiles):
        read(piece).wait()

        for index in range(per_device):
            picked = pick_ref[index]
            sender, slot = lax.div(picked, capacity), lax.rem(picked, capacity)
            staged[piece, :, index * LANES : (index + 1) * LANES] = pieces[piece, sender, slot]
        write(piece).start()
    scale_copy.wait()
    lanes = lax.broadcasted_iota(jnp.int32, (scale_rows, LANES), 1)
    rows_of = lax.broadcasted_iota(jnp.int32, (scale_rows, LANES), 0)

    def gather(index, totals):
        picked = pick_ref[index]
        sender, slot = lax.div(picked, capacity), lax.rem(picked, capacity)
        hit = (lanes == index) & (rows_of // tiles == slot)
        return tuple(
            jnp.where(hit, scale_tiles[half, sender].astype(jnp.float32), totals[half]) for half in range(cores)
        )

    zero = jnp.zeros((scale_rows, LANES), jnp.float32)
    totals = lax.fori_loop(0, per_device, gather, (zero,) * cores)
    for half in range(cores):
        folded = jnp.zeros((tiles, LANES), jnp.float32)
        for slot in range(capacity):
            folded = folded + totals[half][slot * tiles : (slot + 1) * tiles]
        scales_ref[0, half * tiles : (half + 1) * tiles, :] = folded[:, :per_device].astype(jnp.bfloat16)

    for piece in range(cores * tiles):
        write(piece).wait()


def body(weights, block_ids, owner_map):
    shards = lax.axis_size("fsdp")
    cores = lax.axis_size("rep")
    per_device, height, columns = weights.shape
    capacity = (per_device + shards - 1) // shards
    tiles = columns // LANES
    scale_rows = (capacity * tiles + 15) // 16 * 16
    scalars = pl.BlockSpec(memory_space=pltpu.SMEM)
    anywhere = pl.BlockSpec(memory_space=pl.ANY)
    landed, landed_scales = pl.pallas_call(
        functools.partial(exchange_kernel, shards, capacity),
        out_shape=(
            jax.ShapeDtypeStruct((cores, shards, capacity, columns, LANES), jnp.bfloat16),
            jax.ShapeDtypeStruct((cores, shards, scale_rows, LANES), jnp.bfloat16),
        ),
        in_specs=[scalars, scalars, anywhere],
        out_specs=(anywhere, anywhere),
        scratch_shapes=[
            pltpu.VMEM(weights.shape, jnp.bfloat16),
            pltpu.VMEM((shards, capacity, columns, LANES), jnp.bfloat16),
            pltpu.VMEM((shards, scale_rows, LANES), jnp.bfloat16),
            pltpu.SMEM((per_device,), jnp.int32),
            pltpu.SemaphoreType.DMA,
            pltpu.SemaphoreType.DMA((shards, capacity + 1)),
            pltpu.SemaphoreType.DMA((shards, capacity + 1)),
            pltpu.SemaphoreType.DMA((shards, capacity + 1)),
            pltpu.SemaphoreType.DMA((shards, capacity + 1)),
        ],
        compiler_params=pltpu.CompilerParams(
            collective_id=0, has_side_effects=True, vmem_limit_bytes=60 * 1024 * 1024
        ),
        name="exchange",
    )(block_ids, owner_map, weights)
    return pl.pallas_call(
        place_kernel,
        out_shape=(
            jax.ShapeDtypeStruct((1, cores * columns, per_device * height), jnp.bfloat16),
            jax.ShapeDtypeStruct((1, cores * tiles, per_device), jnp.bfloat16),
        ),
        in_specs=[scalars, scalars, anywhere, anywhere],
        out_specs=(anywhere, pl.BlockSpec(memory_space=pltpu.VMEM)),
        scratch_shapes=[
            pltpu.VMEM((cores * tiles, shards, capacity, LANES, LANES), jnp.bfloat16),
            pltpu.VMEM((cores * tiles, LANES, per_device * height), jnp.bfloat16),
            pltpu.VMEM((cores, shards, scale_rows, LANES), jnp.bfloat16),
            pltpu.SMEM((per_device + 1,), jnp.int32),
            pltpu.SemaphoreType.DMA((cores * tiles,)),
            pltpu.SemaphoreType.DMA((cores * tiles,)),
            pltpu.SemaphoreType.DMA,
        ],
        compiler_params=pltpu.CompilerParams(vmem_limit_bytes=60 * 1024 * 1024),
        name="place",
    )(block_ids, owner_map, landed, landed_scales)


def solution(mesh):
    return jax.shard_map(
        body,
        mesh=mesh,
        in_specs=(P(("groups", "fsdp"), None, "rep"), P(), P()),
        out_specs=(P(("groups", "fsdp"), None, None), P(("groups", "fsdp"), None, None)),
        check_vma=False,
    )
```

```python
import functools

import jax
import jax.numpy as jnp
from jax import lax
from jax.experimental import pallas as pl
from jax.experimental.pallas import tpu as pltpu
from jax.sharding import PartitionSpec as P

MESH = pl.DeviceIdType.MESH
LANES = 128


def far_first(step, shards):
    distance = (step + 1) // 2
    sign = 1 - 2 * ((step + 1) % 2)
    return (shards // 2 + sign * distance + shards) % shards


def exchange_kernel(
    shards,
    capacity,
    block_ids_ref,
    owner_map_ref,
    weights_ref,
    landed_ref,
    landed_scales_ref,
    held_weights,
    outgoing,
    outgoing_scales,
    owner_of,
    read_sem,
    send_sem,
    recv_sem,
    pass_sem,
    passed_sem,
):
    me = lax.axis_index("fsdp")
    core = lax.axis_index("rep")
    other = 1 - core
    per_device, _, columns = weights_ref.shape
    tiles = columns // LANES
    read = pltpu.make_async_copy(weights_ref, held_weights, read_sem)
    read.start()

    barrier = pltpu.get_barrier_semaphore()

    def greet(step, carry):
        peer = (me + step) % shards
        pl.semaphore_signal(barrier, inc=1, device_id={"fsdp": peer}, device_id_type=MESH)
        return carry

    lax.fori_loop(1, shards, greet, 0)
    pl.semaphore_signal(barrier, inc=1, device_id={"rep": other}, device_id_type=MESH)

    def look_up(index, carry):
        owner_of[index] = owner_map_ref[lax.div(block_ids_ref[me * per_device + index], per_device)]
        return carry

    lax.fori_loop(0, per_device, look_up, 0)
    pl.semaphore_wait(barrier, shards)
    read.wait()

    def sources_for(owner):
        def step(index, carry):
            count, found = carry
            hit = owner_of[index] == owner
            found = tuple(jnp.where(hit & (count == slot), index, old) for slot, old in enumerate(found))
            return count + hit.astype(jnp.int32), found

        zero = jnp.int32(0)
        return lax.fori_loop(0, per_device, step, (zero, (zero,) * capacity))[1]

    def fill(owner, slot, source, scale_tile):
        row_ids = lax.broadcasted_iota(jnp.int32, scale_tile.shape, 0)
        for tile in range(tiles):
            block = held_weights[source, :, tile * LANES : (tile + 1) * LANES].astype(jnp.float32)
            largest = jnp.max(jnp.max(jnp.abs(block), axis=0, keepdims=True), axis=1, keepdims=True)
            scale = (largest + 1e-06).astype(jnp.bfloat16).astype(jnp.float32)
            divided = (block / scale).astype(jnp.bfloat16)
            outgoing[owner, slot, tile * LANES : (tile + 1) * LANES, :] = divided.T
            scale_tile = jnp.where(row_ids == slot * tiles + tile, scale, scale_tile)
        return scale_tile

    def copy(start, landing, part, device, done, arrived):
        if part < capacity:
            start_ref, landing_ref = start[0].at[start[2], part], landing[0].at[landing[2], landing[3], part]
        else:
            start_ref, landing_ref = start[1].at[start[2]], landing[1].at[landing[2], landing[3]]
        return pltpu.make_async_remote_copy(
            src_ref=start_ref,
            dst_ref=landing_ref,
            send_sem=done,
            recv_sem=arrived,
            device_id=device,
            device_id_type=MESH,
        )

    outbox = (outgoing, outgoing_scales)
    landed = (landed_ref, landed_scales_ref)

    def to_owner(owner, part):
        return copy(
            (*outbox, owner), (*landed, core, me), part, {"fsdp": owner}, send_sem.at[owner, part], recv_sem.at[me, part]
        )

    def from_sender(sender, part):
        return copy(
            (*outbox, sender),
            (*landed, core, sender),
            part,
            {"fsdp": sender},
            send_sem.at[sender, part],
            recv_sem.at[sender, part],
        )

    def between_cores(half, sender, part):
        here = (landed_ref.at[half], landed_scales_ref.at[half], sender)
        return copy(
            here,
            (*landed, half, sender),
            part,
            {"rep": other},
            pass_sem.at[sender, part],
            passed_sem.at[sender, part],
        )

    def keep(part):
        if part < capacity:
            start_ref, landing_ref = outgoing.at[me, part], landed_ref.at[core, me, part]
        else:
            start_ref, landing_ref = outgoing_scales.at[me], landed_scales_ref.at[core, me]
        return pltpu.make_async_copy(start_ref, landing_ref, recv_sem.at[me, part])

    def prepare(owner, launch):
        sources = sources_for(owner)
        scale_tile = jnp.zeros(outgoing_scales.shape[1:], jnp.float32)
        for slot in range(capacity):
            scale_tile = fill(owner, slot, sources[slot], scale_tile)
            launch(slot).start()
        outgoing_scales[owner] = scale_tile.astype(jnp.bfloat16)
        launch(capacity).start()

    parts = range(capacity + 1)

    def send(step, carry):
        owner = (me + far_first(step, shards)) % shards
        prepare(owner, functools.partial(to_owner, owner))
        return carry

    lax.fori_loop(0, shards - 1, send, 0)
    prepare(me, keep)
    for part in parts:
        keep(part).wait()
        between_cores(core, me, part).start()

    def forward(step, carry):
        sender = (me - far_first(step, shards) + shards) % shards
        for part in parts:
            from_sender(sender, part).wait_recv()
            between_cores(core, sender, part).start()
        return carry

    lax.fori_loop(0, shards - 1, forward, 0)

    def finish(step, carry):
        peer = (me + step) % shards
        for part in parts:
            to_owner(peer, part).wait_send()
        return carry

    lax.fori_loop(1, shards, finish, 0)

    def finish_core(sender, carry):
        for part in parts:
            between_cores(core, sender, part).wait_send()
            between_cores(other, sender, part).wait_recv()
        return carry

    lax.fori_loop(0, shards, finish_core, 0)


def place_kernel(
    block_ids_ref,
    owner_map_ref,
    landed_ref,
    landed_scales_ref,
    matrix_ref,
    scales_ref,
    pieces,
    staged,
    scale_tiles,
    pick_ref,
    read_sems,
    write_sems,
    scale_sem,
):
    me = lax.axis_index("fsdp")
    cores, shards, capacity, columns, _ = landed_ref.shape
    scale_rows = landed_scales_ref.shape[2]
    per_device = pick_ref.shape[0] - 1
    tiles = columns // LANES

    def read(piece):
        half, tile = piece // tiles, piece % tiles
        return pltpu.make_async_copy(
            landed_ref.at[half, :, :, pl.ds(tile * LANES, LANES), :], pieces.at[piece], read_sems.at[piece]
        )

    def write(piece):
        return pltpu.make_async_copy(
            staged.at[piece], matrix_ref.at[0, pl.ds(piece * LANES, LANES), :], write_sems.at[piece]
        )

    scale_copy = pltpu.make_async_copy(landed_scales_ref, scale_tiles, scale_sem)
    for piece in range(cores * tiles):
        read(piece).start(priority=piece % 2)
    scale_copy.start()

    def find_expert(expert, found):
        return jnp.where(owner_map_ref[expert] == me, expert, found)

    lowest = per_device * lax.fori_loop(0, owner_map_ref.shape[0], find_expert, jnp.int32(0))

    def look_up(sender, carry):
        count = jnp.int32(0)
        for index in range(per_device):
            row = block_ids_ref[sender * per_device + index] - lowest
            hit = (row >= 0) & (row < per_device)
            pick_ref[jnp.where(hit, row, per_device)] = sender * capacity + count
            count = count + hit.astype(jnp.int32)
        return carry

    lax.fori_loop(0, shards, look_up, 0)

    for piece in range(cores * tiles):
        read(piece).wait()

        for index in range(per_device):
            picked = pick_ref[index]
            sender, slot = lax.div(picked, capacity), lax.rem(picked, capacity)
            staged[piece, :, index * LANES : (index + 1) * LANES] = pieces[piece, sender, slot]
        write(piece).start(priority=1)
    scale_copy.wait()
    lanes = lax.broadcasted_iota(jnp.int32, (scale_rows, LANES), 1)
    rows_of = lax.broadcasted_iota(jnp.int32, (scale_rows, LANES), 0)

    def gather(index, totals):
        picked = pick_ref[index]
        sender, slot = lax.div(picked, capacity), lax.rem(picked, capacity)
        hit = (lanes == index) & (rows_of // tiles == slot)
        return tuple(
            jnp.where(hit, scale_tiles[half, sender].astype(jnp.float32), totals[half]) for half in range(cores)
        )

    zero = jnp.zeros((scale_rows, LANES), jnp.float32)
    totals = lax.fori_loop(0, per_device, gather, (zero,) * cores)
    for half in range(cores):
        folded = jnp.zeros((tiles, LANES), jnp.float32)
        for slot in range(capacity):
            folded = folded + totals[half][slot * tiles : (slot + 1) * tiles]
        scales_ref[0, half * tiles : (half + 1) * tiles, :] = folded[:, :per_device].astype(jnp.bfloat16)

    for piece in range(cores * tiles):
        write(piece).wait()


def body(weights, block_ids, owner_map):
    shards = lax.axis_size("fsdp")
    cores = lax.axis_size("rep")
    per_device, height, columns = weights.shape
    capacity = (per_device + shards - 1) // shards
    tiles = columns // LANES
    scale_rows = (capacity * tiles + 15) // 16 * 16
    scalars = pl.BlockSpec(memory_space=pltpu.SMEM)
    anywhere = pl.BlockSpec(memory_space=pl.ANY)
    landed, landed_scales = pl.pallas_call(
        functools.partial(exchange_kernel, shards, capacity),
        out_shape=(
            jax.ShapeDtypeStruct((cores, shards, capacity, columns, LANES), jnp.bfloat16),
            jax.ShapeDtypeStruct((cores, shards, scale_rows, LANES), jnp.bfloat16),
        ),
        in_specs=[scalars, scalars, anywhere],
        out_specs=(anywhere, anywhere),
        scratch_shapes=[
            pltpu.VMEM(weights.shape, jnp.bfloat16),
            pltpu.VMEM((shards, capacity, columns, LANES), jnp.bfloat16),
            pltpu.VMEM((shards, scale_rows, LANES), jnp.bfloat16),
            pltpu.SMEM((per_device,), jnp.int32),
            pltpu.SemaphoreType.DMA,
            pltpu.SemaphoreType.DMA((shards, capacity + 1)),
            pltpu.SemaphoreType.DMA((shards, capacity + 1)),
            pltpu.SemaphoreType.DMA((shards, capacity + 1)),
            pltpu.SemaphoreType.DMA((shards, capacity + 1)),
        ],
        compiler_params=pltpu.CompilerParams(
            collective_id=0, has_side_effects=True, vmem_limit_bytes=60 * 1024 * 1024
        ),
        name="exchange",
    )(block_ids, owner_map, weights)
    return pl.pallas_call(
        place_kernel,
        out_shape=(
            jax.ShapeDtypeStruct((1, cores * columns, per_device * height), jnp.bfloat16),
            jax.ShapeDtypeStruct((1, cores * tiles, per_device), jnp.bfloat16),
        ),
        in_specs=[scalars, scalars, anywhere, anywhere],
        out_specs=(anywhere, pl.BlockSpec(memory_space=pltpu.VMEM)),
        scratch_shapes=[
            pltpu.VMEM((cores * tiles, shards, capacity, LANES, LANES), jnp.bfloat16),
            pltpu.VMEM((cores * tiles, LANES, per_device * height), jnp.bfloat16),
            pltpu.VMEM((cores, shards, scale_rows, LANES), jnp.bfloat16),
            pltpu.SMEM((per_device + 1,), jnp.int32),
            pltpu.SemaphoreType.DMA((cores * tiles,)),
            pltpu.SemaphoreType.DMA((cores * tiles,)),
            pltpu.SemaphoreType.DMA,
        ],
        compiler_params=pltpu.CompilerParams(vmem_limit_bytes=60 * 1024 * 1024),
        name="place",
    )(block_ids, owner_map, landed, landed_scales)


def solution(mesh):
    return jax.shard_map(
        body,
        mesh=mesh,
        in_specs=(P(("groups", "fsdp"), None, "rep"), P(), P()),
        out_specs=(P(("groups", "fsdp"), None, None), P(("groups", "fsdp"), None, None)),
        check_vma=False,
    )
```

```python
import functools

import jax
import jax.numpy as jnp
from jax import lax
from jax.experimental import pallas as pl
from jax.experimental.pallas import tpu as pltpu
from jax.sharding import PartitionSpec as P

MESH = pl.DeviceIdType.MESH
LANES = 128


def far_first(step, shards):
    distance = (step + 1) // 2
    sign = 1 - 2 * ((step + 1) % 2)
    return (shards // 2 + sign * distance + shards) % shards


def exchange_kernel(
    shards,
    capacity,
    block_ids_ref,
    owner_map_ref,
    weights_ref,
    landed_ref,
    landed_scales_ref,
    held_weights,
    outgoing,
    outgoing_scales,
    owner_of,
    read_sem,
    send_sem,
    recv_sem,
    pass_sem,
    passed_sem,
):
    me = lax.axis_index("fsdp")
    core = lax.axis_index("rep")
    other = 1 - core
    per_device, _, columns = weights_ref.shape
    tiles = columns // LANES
    middle = per_device // 2
    reads = [
        pltpu.make_async_copy(weights_ref.at[part], held_weights.at[part], read_sem.at[queue])
        for queue, part in enumerate((pl.ds(0, middle), pl.ds(middle, per_device - middle)))
    ]
    for queue, read in enumerate(reads):
        read.start(priority=queue)

    barrier = pltpu.get_barrier_semaphore()

    def greet(step, carry):
        peer = (me + step) % shards
        pl.semaphore_signal(barrier, inc=1, device_id={"fsdp": peer}, device_id_type=MESH)
        return carry

    lax.fori_loop(1, shards, greet, 0)
    pl.semaphore_signal(barrier, inc=1, device_id={"rep": other}, device_id_type=MESH)

    def look_up(index, carry):
        owner_of[index] = owner_map_ref[lax.div(block_ids_ref[me * per_device + index], per_device)]
        return carry

    lax.fori_loop(0, per_device, look_up, 0)
    pl.semaphore_wait(barrier, shards)
    for read in reads:
        read.wait()

    def sources_for(owner):
        def step(index, carry):
            count, found = carry
            hit = owner_of[index] == owner
            found = tuple(jnp.where(hit & (count == slot), index, old) for slot, old in enumerate(found))
            return count + hit.astype(jnp.int32), found

        zero = jnp.int32(0)
        return lax.fori_loop(0, per_device, step, (zero, (zero,) * capacity))[1]

    def fill(owner, slot, source, scale_tile):
        row_ids = lax.broadcasted_iota(jnp.int32, scale_tile.shape, 0)
        for tile in range(tiles):
            block = held_weights[source, :, tile * LANES : (tile + 1) * LANES].astype(jnp.float32)
            largest = jnp.max(jnp.max(jnp.abs(block), axis=0, keepdims=True), axis=1, keepdims=True)
            scale = (largest + 1e-06).astype(jnp.bfloat16).astype(jnp.float32)
            divided = (block / scale).astype(jnp.bfloat16)
            outgoing[owner, slot, tile * LANES : (tile + 1) * LANES, :] = divided.T
            scale_tile = jnp.where(row_ids == slot * tiles + tile, scale, scale_tile)
        return scale_tile

    def copy(start, landing, part, device, done, arrived):
        if part < capacity:
            start_ref, landing_ref = start[0].at[start[2], part], landing[0].at[landing[2], landing[3], part]
        else:
            start_ref, landing_ref = start[1].at[start[2]], landing[1].at[landing[2], landing[3]]
        return pltpu.make_async_remote_copy(
            src_ref=start_ref,
            dst_ref=landing_ref,
            send_sem=done,
            recv_sem=arrived,
            device_id=device,
            device_id_type=MESH,
        )

    outbox = (outgoing, outgoing_scales)
    landed = (landed_ref, landed_scales_ref)

    def to_owner(owner, part):
        return copy(
            (*outbox, owner), (*landed, core, me), part, {"fsdp": owner}, send_sem.at[owner, part], recv_sem.at[me, part]
        )

    def from_sender(sender, part):
        return copy(
            (*outbox, sender),
            (*landed, core, sender),
            part,
            {"fsdp": sender},
            send_sem.at[sender, part],
            recv_sem.at[sender, part],
        )

    def between_cores(half, sender, part):
        here = (landed_ref.at[half], landed_scales_ref.at[half], sender)
        return copy(
            here,
            (*landed, half, sender),
            part,
            {"rep": other},
            pass_sem.at[sender, part],
            passed_sem.at[sender, part],
        )

    def keep(part):
        if part < capacity:
            start_ref, landing_ref = outgoing.at[me, part], landed_ref.at[core, me, part]
        else:
            start_ref, landing_ref = outgoing_scales.at[me], landed_scales_ref.at[core, me]
        return pltpu.make_async_copy(start_ref, landing_ref, recv_sem.at[me, part])

    def prepare(owner, launch):
        sources = sources_for(owner)
        scale_tile = jnp.zeros(outgoing_scales.shape[1:], jnp.float32)
        for slot in range(capacity):
            scale_tile = fill(owner, slot, sources[slot], scale_tile)
            launch(slot).start()
        outgoing_scales[owner] = scale_tile.astype(jnp.bfloat16)
        launch(capacity).start()

    parts = range(capacity + 1)

    def send(step, carry):
        owner = (me + far_first(step, shards)) % shards
        prepare(owner, functools.partial(to_owner, owner))
        return carry

    lax.fori_loop(0, shards - 1, send, 0)
    prepare(me, keep)
    for part in parts:
        keep(part).wait()
        between_cores(core, me, part).start()

    def forward(step, carry):
        sender = (me - far_first(step, shards) + shards) % shards
        for part in parts:
            from_sender(sender, part).wait_recv()
            between_cores(core, sender, part).start()
        return carry

    lax.fori_loop(0, shards - 1, forward, 0)

    def finish(step, carry):
        peer = (me + step) % shards
        for part in parts:
            to_owner(peer, part).wait_send()
        return carry

    lax.fori_loop(1, shards, finish, 0)

    def finish_core(sender, carry):
        for part in parts:
            between_cores(core, sender, part).wait_send()
            between_cores(other, sender, part).wait_recv()
        return carry

    lax.fori_loop(0, shards, finish_core, 0)


def place_kernel(
    block_ids_ref,
    owner_map_ref,
    landed_ref,
    landed_scales_ref,
    matrix_ref,
    scales_ref,
    pieces,
    staged,
    scale_tiles,
    pick_ref,
    read_sems,
    write_sems,
    scale_sem,
):
    me = lax.axis_index("fsdp")
    cores, shards, capacity, columns, _ = landed_ref.shape
    scale_rows = landed_scales_ref.shape[2]
    per_device = pick_ref.shape[0] - 1
    tiles = columns // LANES

    def read(piece, queue):
        senders = pl.ds(queue * (shards // 2), shards // 2)
        half, tile = piece // tiles, piece % tiles
        return pltpu.make_async_copy(
            landed_ref.at[half, senders, :, pl.ds(tile * LANES, LANES), :],
            pieces.at[piece, senders],
            read_sems.at[piece, queue],
        )

    def write(piece):
        return pltpu.make_async_copy(
            staged.at[piece], matrix_ref.at[0, pl.ds(piece * LANES, LANES), :], write_sems.at[piece]
        )

    scale_copy = pltpu.make_async_copy(landed_scales_ref, scale_tiles, scale_sem)
    for piece in range(cores * tiles):
        for queue in range(2):
            read(piece, queue).start(priority=queue)
    scale_copy.start()

    def find_expert(expert, found):
        return jnp.where(owner_map_ref[expert] == me, expert, found)

    lowest = per_device * lax.fori_loop(0, owner_map_ref.shape[0], find_expert, jnp.int32(0))

    def look_up(sender, carry):
        count = jnp.int32(0)
        for index in range(per_device):
            row = block_ids_ref[sender * per_device + index] - lowest
            hit = (row >= 0) & (row < per_device)
            pick_ref[jnp.where(hit, row, per_device)] = sender * capacity + count
            count = count + hit.astype(jnp.int32)
        return carry

    lax.fori_loop(0, shards, look_up, 0)

    for piece in range(cores * tiles):
        for queue in range(2):
            read(piece, queue).wait()

        for index in range(per_device):
            picked = pick_ref[index]
            sender, slot = lax.div(picked, capacity), lax.rem(picked, capacity)
            staged[piece, :, index * LANES : (index + 1) * LANES] = pieces[piece, sender, slot]
        write(piece).start(priority=1)
    scale_copy.wait()
    lanes = lax.broadcasted_iota(jnp.int32, (scale_rows, LANES), 1)
    rows_of = lax.broadcasted_iota(jnp.int32, (scale_rows, LANES), 0)

    def gather(index, totals):
        picked = pick_ref[index]
        sender, slot = lax.div(picked, capacity), lax.rem(picked, capacity)
        hit = (lanes == index) & (rows_of // tiles == slot)
        return tuple(
            jnp.where(hit, scale_tiles[half, sender].astype(jnp.float32), totals[half]) for half in range(cores)
        )

    zero = jnp.zeros((scale_rows, LANES), jnp.float32)
    totals = lax.fori_loop(0, per_device, gather, (zero,) * cores)
    for half in range(cores):
        folded = jnp.zeros((tiles, LANES), jnp.float32)
        for slot in range(capacity):
            folded = folded + totals[half][slot * tiles : (slot + 1) * tiles]
        scales_ref[0, half * tiles : (half + 1) * tiles, :] = folded[:, :per_device].astype(jnp.bfloat16)

    for piece in range(cores * tiles):
        write(piece).wait()


def body(weights, block_ids, owner_map):
    shards = lax.axis_size("fsdp")
    cores = lax.axis_size("rep")
    per_device, height, columns = weights.shape
    capacity = (per_device + shards - 1) // shards
    tiles = columns // LANES
    scale_rows = (capacity * tiles + 15) // 16 * 16
    scalars = pl.BlockSpec(memory_space=pltpu.SMEM)
    anywhere = pl.BlockSpec(memory_space=pl.ANY)
    landed, landed_scales = pl.pallas_call(
        functools.partial(exchange_kernel, shards, capacity),
        out_shape=(
            jax.ShapeDtypeStruct((cores, shards, capacity, columns, LANES), jnp.bfloat16),
            jax.ShapeDtypeStruct((cores, shards, scale_rows, LANES), jnp.bfloat16),
        ),
        in_specs=[scalars, scalars, anywhere],
        out_specs=(anywhere, anywhere),
        scratch_shapes=[
            pltpu.VMEM(weights.shape, jnp.bfloat16),
            pltpu.VMEM((shards, capacity, columns, LANES), jnp.bfloat16),
            pltpu.VMEM((shards, scale_rows, LANES), jnp.bfloat16),
            pltpu.SMEM((per_device,), jnp.int32),
            pltpu.SemaphoreType.DMA((2,)),
            pltpu.SemaphoreType.DMA((shards, capacity + 1)),
            pltpu.SemaphoreType.DMA((shards, capacity + 1)),
            pltpu.SemaphoreType.DMA((shards, capacity + 1)),
            pltpu.SemaphoreType.DMA((shards, capacity + 1)),
        ],
        compiler_params=pltpu.CompilerParams(
            collective_id=0, has_side_effects=True, vmem_limit_bytes=60 * 1024 * 1024
        ),
        name="exchange",
    )(block_ids, owner_map, weights)
    return pl.pallas_call(
        place_kernel,
        out_shape=(
            jax.ShapeDtypeStruct((1, cores * columns, per_device * height), jnp.bfloat16),
            jax.ShapeDtypeStruct((1, cores * tiles, per_device), jnp.bfloat16),
        ),
        in_specs=[scalars, scalars, anywhere, anywhere],
        out_specs=(anywhere, pl.BlockSpec(memory_space=pltpu.VMEM)),
        scratch_shapes=[
            pltpu.VMEM((cores * tiles, shards, capacity, LANES, LANES), jnp.bfloat16),
            pltpu.VMEM((cores * tiles, LANES, per_device * height), jnp.bfloat16),
            pltpu.VMEM((cores, shards, scale_rows, LANES), jnp.bfloat16),
            pltpu.SMEM((per_device + 1,), jnp.int32),
            pltpu.SemaphoreType.DMA((cores * tiles, 2)),
            pltpu.SemaphoreType.DMA((cores * tiles,)),
            pltpu.SemaphoreType.DMA,
        ],
        compiler_params=pltpu.CompilerParams(vmem_limit_bytes=60 * 1024 * 1024),
        name="place",
    )(block_ids, owner_map, landed, landed_scales)


def solution(mesh):
    return jax.shard_map(
        body,
        mesh=mesh,
        in_specs=(P(("groups", "fsdp"), None, "rep"), P(), P()),
        out_specs=(P(("groups", "fsdp"), None, None), P(("groups", "fsdp"), None, None)),
        check_vma=False,
    )
```
